32 devices in a mesh: row: 8 (over y, x, core), help: 4 (over z).
Axes of the slice: x: 2, y: 2, z: 4, core: 2. Of those that a mesh axis runs over, the one named last changes fastest.
Arguments:
- points: float32 [32, 4, 1024], P(('row', 'help')), as said below
- sketch: bfloat16 [8, 4, 8, 2, 1024, 256], P('row', 'help'), may hold values from -6 to 6
- slots: int32 [8, 4, 8, 2], P('row', 'help'), may hold values from -1 to 3, as said below
- ranks: int32 [32], P(('row', 'help')), may hold values from 32 to 256
Outputs:
- block_row_sketches: float32 [32, 1024, 256], P(('row', 'help'))
- gram: float32 [32, 256, 256], P(('row', 'help'))
The draws below stay inside these ranges and needn't reach their ends.
Inputs may be any that keep to these rules, and one draw needn't show every extreme that they name: For c = group * 4 + column, each of points[c, 0:3] lies within 1.5 of the matching coordinate of (column / 4, (group % 4) / 4, (group // 4) / 4); points[c, 3] lie in [0.05, 1]. `slots`: a named column differs from the source's column c; the 2 entries [g, c, r, :] that are named differ; for some c and r all 16 entries [:, c, r, :] are named.
All inputs are finite; a program needn't handle non-finite values.
Results may differ from the reference program's by a relative error of at most 0.0029.
Values may be sent and summed in bfloat16 or wider, within the bound.
A program may use at most 128 MiB of HBM per device.

```python
import jax
import jax.numpy as jnp
from jax import lax

PANELS = 1024
SKETCH = 256
SLOTS = 2
GROUPS = 8
HELPERS = 4
CLUSTERS = 32


def draw_points(key, part):
    key_jitter = jax.random.fold_in(key, 11)
    key_area = jax.random.fold_in(key, 12)
    cluster = jnp.arange(CLUSTERS, dtype=jnp.int32)
    group = cluster // HELPERS
    column_index = cluster % HELPERS
    centre = jnp.stack([column_index.astype(jnp.float32) / HELPERS, (group % 4).astype(jnp.float32) / 4.0, (group // 4).astype(jnp.float32) / 4.0], axis=1)
    jitter = jax.random.uniform(key_jitter, (CLUSTERS, 3, PANELS), jnp.float32, -1.5, 1.5)
    coords = centre[:, :, None] + jitter
    area = jnp.exp(jax.random.uniform(key_area, (CLUSTERS, 1, PANELS), jnp.float32, jnp.log(0.05), 0.0))
    return jnp.concatenate([coords, area], axis=1)


def draw_slots(key, part):
    initial_key = jax.random.fold_in(key, 21)
    key_second = jax.random.fold_in(key, 22)
    key_level = jax.random.fold_in(key, 23)
    key_forced = jax.random.fold_in(key, 24)
    active_key = jax.random.fold_in(key, 25)
    shape = (GROUPS, HELPERS, GROUPS)
    column_index = jnp.arange(HELPERS, dtype=jnp.int32)[None, :, None]
    first_step = jax.random.randint(initial_key, shape, 0, HELPERS - 1)
    second_step = jax.random.randint(key_second, shape, 0, HELPERS - 2)
    first = (column_index + 1 + first_step) % HELPERS
    second = (column_index + 1 + (first_step + 1 + second_step) % (HELPERS - 1)) % HELPERS
    chosen = jnp.stack([first, second], axis=3)
    level = jax.random.randint(key_level, (HELPERS, GROUPS), 1, 9)
    forced = jax.random.randint(key_forced, (), 0, HELPERS * GROUPS)
    flat_index = jnp.arange(HELPERS * GROUPS, dtype=jnp.int32).reshape(HELPERS, GROUPS)
    level = jnp.where(flat_index == forced, 10, level)
    alive = jax.random.randint(active_key, (GROUPS, HELPERS, GROUPS, SLOTS), 0, 10) < level[None, :, :, None]
    return jnp.where(alive, chosen, -1).astype(jnp.int32)


def set_ends(array, stream_key, smallest, top_value):
    extent = array.shape
    place = [jax.random.randint(jax.random.fold_in(stream_key, axis), (), 0, extent[axis]) for axis in range(len(extent))]
    array = array.at[tuple(place)].set(smallest)
    longest = extent.index(max(extent))
    place[longest] = (place[longest] + 1) % extent[longest]
    return array.at[tuple(place)].set(top_value)


def block_scale(own_key, extent, split, smallest, largest):
    def one(dim, shards_of):
        heights = jax.random.uniform(jax.random.fold_in(jax.random.fold_in(own_key, 6), dim), (shards_of,), jnp.float32, smallest / len(split), largest / len(split))
        return jnp.repeat(jnp.exp(heights), extent[dim] // shards_of).reshape((-1,) + (1,) * (len(extent) - dim - 1))

    factor_of = one(*split[0])
    for cut in split[1:]:
        factor_of = factor_of * one(*cut)
    return factor_of


def normal_values(stream_key, extent, deviation, limit, pieces=(), kind=jnp.bfloat16):
    gain = block_scale(stream_key, extent, pieces, -0.22, 0.18) if pieces else 1.0
    drawn = jax.random.normal(stream_key, extent, jnp.float32) * deviation * gain
    return jnp.minimum(jnp.maximum(drawn, -limit), limit).astype(kind)


def setup_inputs(seed: int = 0) -> dict:
    key_of = jax.random.split(jax.random.key(seed), 5)
    points = draw_points(jax.random.fold_in(key_of[4], 71), 0)
    sketch = normal_values(key_of[1], (GROUPS, HELPERS, GROUPS, SLOTS, PANELS, SKETCH), 1.0, 6.0, ((0, 8), (1, 4)))
    slots = draw_slots(jax.random.fold_in(key_of[4], 71), 0)
    ranks = set_ends(jax.random.randint(key_of[3], (CLUSTERS,), SKETCH // 8, SKETCH + 1), jax.random.fold_in(key_of[3], 1), SKETCH // 8, SKETCH).astype(jnp.int32)
    return dict(points=points, sketch=sketch, slots=slots, ranks=ranks)


decay_rate = 0.3
four_pi = 12.566370614359172
soften = 0.0025

def kernel_tile(target, source):
    offset_along_x = target[0][:, None] - source[0][None, :]
    delta_y = target[1][:, None] - source[1][None, :]
    offset_along_z = target[2][:, None] - source[2][None, :]
    distance = jnp.sqrt(offset_along_x * offset_along_x + delta_y * delta_y + offset_along_z * offset_along_z + soften)
    values = jnp.exp(-decay_rate * distance) / (four_pi * distance) * source[3][None, :]
    return values.astype(jnp.bfloat16)

def reference(points, sketch, slots, ranks):
    total = GROUPS * HELPERS * GROUPS * SLOTS
    flat_sketch = sketch.reshape(total, PANELS, SKETCH)
    flat_slots = slots.reshape(total).astype(jnp.int32)

    def step(index, sums):
        index = jnp.asarray(index, jnp.int32)
        anchor_cluster_group = index // (HELPERS * GROUPS * SLOTS)
        anchor_column = index // (GROUPS * SLOTS) % HELPERS
        target_group = index // SLOTS % GROUPS
        column_index = flat_slots[index]
        alive = column_index >= 0
        target = (target_group * HELPERS + jnp.maximum(column_index, 0)).astype(jnp.int32)
        source = (anchor_cluster_group * HELPERS + anchor_column).astype(jnp.int32)
        tile = kernel_tile(lax.dynamic_index_in_dim(points, target, 0, keepdims=False), lax.dynamic_index_in_dim(points, source, 0, keepdims=False))
        block = lax.dynamic_index_in_dim(flat_sketch, index, 0, keepdims=False)
        product = jnp.dot(tile, block, preferred_element_type=jnp.float32)
        product = jnp.where(alive, product, jnp.zeros_like(product))
        current = lax.dynamic_index_in_dim(sums, target, 0, keepdims=True)
        return lax.dynamic_update_index_in_dim(sums, current + product[None], target, 0)
    sums = lax.fori_loop(0, total, step, jnp.zeros((CLUSTERS, PANELS, SKETCH), jnp.float32))
    keep = jnp.arange(SKETCH, dtype=jnp.int32)[None, None, :] < ranks[:, None, None]
    block_row_sketches = jnp.where(keep, sums, jnp.zeros_like(sums))
    gram = jnp.einsum('usv,usw->uvw', block_row_sketches, block_row_sketches, precision=lax.Precision.HIGHEST)
    return (block_row_sketches, gram)
```

```python
import functools

import jax
import jax.numpy as jnp
from jax import lax
from jax.experimental import pallas as pl
from jax.experimental.pallas import tpu as pltpu
from jax.sharding import PartitionSpec as P

decay_rate = 0.3
four_pi = 12.566370614359172
soften = 0.0025
log2_e = 1.4426950408889634
centre = 0.4
MESH = pl.DeviceIdType.MESH


def cut(value):
    first = lax.reduce_precision(value, 8, 7)
    rest = value - first
    second = lax.reduce_precision(rest, 8, 7)
    third = lax.reduce_precision(rest - second, 8, 7)
    return first, second, third


def kernel(
    sizes,
    sketch_ref, spots_ref, feats_ref, logw_ref, hot_ref,
    sums_ref,
    sk_own, sk_got, spots, feats_got, logw_got, hot_got,
    lhs, acc, q_send, q_recv, q_own, z_send, z_recv,
    own_sem, sk_send_sem, sk_recv_sem, spot_send_sem, spot_recv_sem,
    side_send_sem, side_recv_sem, q_send_sem, q_recv_sem, z_send_sem, z_recv_sem,
):
    chips, helpers, slots, chunk, chunks, width = sizes
    others = helpers - 1
    row = lax.axis_index("row")
    col = lax.axis_index("help")
    chip, core = row // 2, row % 2
    sibling = chip * 2 + 1 - core
    peers = chips * helpers

    def place(step):
        return (lax.rem(chip + step // helpers, chips), lax.rem(col + step % helpers, helpers))

    def back(step):
        return (
            lax.rem(chip + chips - step // helpers, chips),
            lax.rem(col + helpers - step % helpers, helpers),
        )

    barrier = pltpu.get_barrier_semaphore()

    @pl.loop(1, peers)
    def _(step):
        to_chip, to_col = place(step)
        pl.semaphore_signal(barrier, inc=1, device_id=(to_chip * 2 + core, to_col), device_id_type=MESH)

    pl.semaphore_signal(barrier, inc=1, device_id=(sibling, col), device_id_type=MESH)
    pl.semaphore_wait(barrier, peers)

    def spot_copy(step):
        to_chip, to_col = place(step)
        return pltpu.make_async_remote_copy(
            src_ref=spots_ref,
            dst_ref=spots.at[chip * helpers + col],
            send_sem=spot_send_sem.at[step],
            recv_sem=spot_recv_sem.at[step],
            device_id=(to_chip * 2 + core, to_col),
            device_id_type=MESH,
        )

    def spot_arrival(step):
        from_chip, from_col = back(step)
        return pltpu.make_async_remote_copy(
            src_ref=spots_ref,
            dst_ref=spots.at[from_chip * helpers + from_col],
            send_sem=spot_send_sem.at[step],
            recv_sem=spot_recv_sem.at[step],
            device_id=(from_chip * 2 + core, from_col),
            device_id_type=MESH,
        )

    def to_sibling(source, target, index):
        return pltpu.make_async_remote_copy(
            src_ref=source,
            dst_ref=target,
            send_sem=side_send_sem.at[index],
            recv_sem=side_recv_sem.at[index],
            device_id=(sibling, col),
            device_id_type=MESH,
        )

    sides = (
        to_sibling(feats_ref, feats_got, 0),
        to_sibling(logw_ref, logw_got, 1),
        to_sibling(hot_ref.at[:, 1 - core], hot_got, 2),
    )

    def sketch_copy(offset):
        group = lax.rem(chip + offset, chips)
        return pltpu.make_async_remote_copy(
            src_ref=sketch_ref.at[group, 1 - core],
            dst_ref=sk_got.at[group],
            send_sem=sk_send_sem.at[offset],
            recv_sem=sk_recv_sem.at[offset],
            device_id=(sibling, col),
            device_id_type=MESH,
        )

    def own_copy(offset):
        group = lax.rem(chip + offset, chips)
        return pltpu.make_async_copy(sketch_ref.at[group, core], sk_own.at[group], own_sem.at[offset])

    own_spot = pltpu.make_async_copy(spots_ref, spots.at[chip * helpers + col], own_sem.at[chips])
    own_spot.start()

    @pl.loop(1, peers)
    def _(step):
        spot_copy(step).start()

    for side in sides:
        side.start()

    @pl.loop(0, chips)
    def _(turn):
        offset = chips - 1 - turn
        sketch_copy(offset).start()
        own_copy(offset).start()

    lhs[...] = jnp.where(
        lax.broadcasted_iota(jnp.int32, lhs.shape, 1) == 4, jnp.float32(1), jnp.float32(0)
    )
    own_spot.wait()
    for side in sides:
        side.wait()

    @pl.loop(1, peers)
    def _(step):
        spot_copy(step).wait_send()
        spot_arrival(step).wait_recv()

    def q_copy(index, offset):
        to_chip = lax.rem(chip + offset, chips)
        return pltpu.make_async_remote_copy(
            src_ref=q_send.at[index % 2, offset - 1],
            dst_ref=q_recv.at[index, offset - 1],
            send_sem=q_send_sem.at[index % 2, offset - 1],
            recv_sem=q_recv_sem.at[index, offset - 1],
            device_id=(to_chip * 2 + core, col),
            device_id_type=MESH,
        )

    def z_copy(index, step):
        return pltpu.make_async_remote_copy(
            src_ref=z_send.at[index, step],
            dst_ref=z_recv.at[index, step],
            send_sem=z_send_sem.at[index, step],
            recv_sem=z_recv_sem.at[index, step],
            device_id=(row, lax.rem(col + 1 + step, helpers)),
            device_id_type=MESH,
        )

    def block(index, group, sketches, feats, logw, hot_rows, slot, first):
        rows = pl.ds(pl.multiple_of(index * chunk, chunk), chunk)
        spot = jnp.zeros((4, chunk), jnp.float32)
        hots = []
        for step in range(others):
            hot = hot_rows(slot * others + step)
            hots.append(hot)
            target = group * helpers + lax.rem(col + 1 + step, helpers)
            spot = spot + hot[:, :chunk] * spots[target, :, rows]
        lhs[slot if first else slots + slot, 0:4, :] = spot
        full = lhs[slot if first else slots + slot]
        one = full.astype(jnp.bfloat16).astype(jnp.float32)
        rest = full - one
        two = rest.astype(jnp.bfloat16).astype(jnp.float32)
        three = rest - two
        stack = jnp.concatenate([one, one, two, two, one, three], axis=0)
        left = stack.T.astype(jnp.bfloat16)
        square = jnp.dot(left, feats, preferred_element_type=jnp.float32)
        inverse = lax.rsqrt(square)
        tile = (jnp.exp2(logw - square * inverse) * inverse).astype(jnp.bfloat16)
        product = jnp.dot(tile, sketches, preferred_element_type=jnp.float32)
        return [hot[:, :width] * product for hot in hots]

    def compute(index, offset):
        group = lax.rem(chip + offset, chips)
        totals = [None] * others
        for slot in range(slots):
            for first in (True, False):
                if first:
                    parts = block(
                        index, group, sk_own[group, slot], feats_ref[...], logw_ref[...],
                        lambda place: hot_ref[group, core, place], slot, True,
                    )
                else:
                    parts = block(
                        index, group, sk_got[group, slot], feats_got[...], logw_got[...],
                        lambda place: hot_got[group, place], slot, False,
                    )
                for step in range(others):
                    totals[step] = parts[step] if totals[step] is None else totals[step] + parts[step]
        for step in range(others):
            acc[step] = totals[step]

    def gather(index):
        @pl.loop(1, chips)
        def _(offset):
            q_copy(index, offset).wait_recv()

        for step in range(others):
            def add(offset, total):
                return total + q_recv[index, offset, step].astype(jnp.float32)

            total = lax.fori_loop(0, chips - 1, add, q_own[index % 2, step])
            z_send[index, step] = total.astype(jnp.bfloat16)
            z_copy(index, step).start()

    def finish(index):
        total = None
        for step in range(others):
            z_copy(index, step).wait_recv()
            part = z_recv[index, step].astype(jnp.float32)
            total = part if total is None else total + part
        rows = pl.ds(pl.multiple_of(index * chunk, chunk), chunk)
        sums_ref[rows, :] = total

    @pl.loop(0, chunks)
    def _(index):
        @pl.loop(0, chips)
        def _(turn):
            offset = chips - 1 - turn

            @pl.when(index == 0)
            def _():
                own_copy(offset).wait()
                sketch_copy(offset).wait()

            compute(index, offset)

            @pl.when(offset > 0)
            def _():
                @pl.when(index >= 2)
                def _():
                    q_copy(index, offset).wait_send()

                for step in range(others):
                    q_send[index % 2, offset - 1, step] = acc[step].astype(jnp.bfloat16)
                q_copy(index, offset).start()

            @pl.when(offset == 0)
            def _():
                for step in range(others):
                    q_own[index % 2, step] = acc[step]

        @pl.when(index >= 1)
        def _():
            gather(index - 1)

        @pl.when(index >= 2)
        def _():
            finish(index - 2)

    gather(chunks - 1)
    finish(chunks - 2)
    finish(chunks - 1)

    for index in (chunks - 2, chunks - 1):
        @pl.loop(1, chips)
        def _(offset):
            q_copy(index, offset).wait_send()

    @pl.loop(0, chunks)
    def _(index):
        for step in range(others):
            z_copy(index, step).wait_send()


def per_device(points, sketch, slots, ranks):
    panels = points.shape[2]
    width = sketch.shape[5]
    groups = sketch.shape[2]
    count = sketch.shape[3]
    helpers = lax.axis_size("help")
    others = helpers - 1
    chips = groups // 2
    chunk = panels // 4 if groups <= 8 else panels // 8
    chunks = panels // chunk
    col = lax.axis_index("help")

    scale = decay_rate * log2_e
    spot = (points[0, 0:3] - centre) * scale
    norm = jnp.sum(spot * spot, axis=0, keepdims=True)
    spots = jnp.concatenate([spot, norm], axis=0)
    blank = jnp.zeros((3, panels), jnp.float32)
    right = jnp.concatenate(
        [-2.0 * spot, jnp.ones((1, panels), jnp.float32), norm + soften * scale * scale, blank], axis=0
    )
    one, two, three = cut(right)
    feats = jnp.concatenate([one, two, one, two, three, one], axis=0).astype(jnp.bfloat16)
    logw = jnp.log2(points[0, 3:4]) + jnp.log2(jnp.float32(scale / four_pi))
    step = jnp.where(slots[0, 0] >= 0, (slots[0, 0] - col - 1) % helpers, -1)
    hot = (step[:, :, None] == jnp.arange(others, dtype=jnp.int32)).astype(jnp.float32)
    span = max(width, chunk)
    hot = jnp.broadcast_to(
        hot.reshape(chips, 2, count * others, 1, 1), (chips, 2, count * others, 1, span)
    )
    sizes = (chips, helpers, count, chunk, chunks, width)
    bf16, f32 = jnp.bfloat16, jnp.float32
    vmem = pl.BlockSpec(memory_space=pltpu.VMEM)
    dma = pltpu.SemaphoreType.DMA
    sums = pl.pallas_call(
        functools.partial(kernel, sizes),
        out_shape=jax.ShapeDtypeStruct((panels, width), f32),
        in_specs=[pl.BlockSpec(memory_space=pl.ANY), vmem, vmem, vmem, vmem],
        out_specs=vmem,
        scratch_shapes=[
            pltpu.VMEM((chips, count, panels, width), bf16),
            pltpu.VMEM((chips, count, panels, width), bf16),
            pltpu.VMEM((chips * helpers, 4, panels), f32),
            pltpu.VMEM((48, panels), bf16),
            pltpu.VMEM((1, panels), f32),
            pltpu.VMEM((chips, count * others, 1, span), f32),
            pltpu.VMEM((2 * count, 8, chunk), f32),
            pltpu.VMEM((others, chunk, width), f32),
            pltpu.VMEM((2, chips - 1, others, chunk, width), bf16),
            pltpu.VMEM((chunks, chips - 1, others, chunk, width), bf16),
            pltpu.VMEM((2, others, chunk, width), f32),
            pltpu.VMEM((chunks, others, chunk, width), bf16),
            pltpu.VMEM((chunks, others, chunk, width), bf16),
            dma((chips + 1,)),
            dma((chips,)),
            dma((chips,)),
            dma((chips * helpers,)),
            dma((chips * helpers,)),
            dma((3,)),
            dma((3,)),
            dma((2, chips - 1)),
            dma((chunks, chips - 1)),
            dma((chunks, others)),
            dma((chunks, others)),
        ],
        compiler_params=pltpu.CompilerParams(
            collective_id=0, has_side_effects=True, vmem_limit_bytes=60 * 1024 * 1024
        ),
    )(
        sketch.reshape(chips, 2, count, panels, width), spots, feats, logw, hot,
    )
    keep = jnp.arange(width, dtype=jnp.int32)[None, :] < ranks[0]
    kept = jnp.where(keep, sums, jnp.zeros_like(sums))[None]
    gram = jnp.einsum("usv,usw->uvw", kept, kept, precision=lax.Precision.HIGHEST)
    return kept, gram


def solution(mesh):
    in_specs = (
        P(("row", "help"), None, None),
        P("row", "help", None, None, None, None),
        P("row", "help", None, None),
        P(("row", "help")),
    )
    out_specs = (P(("row", "help"), None, None), P(("row", "help"), None, None))
    return jax.shard_map(
        per_device, mesh=mesh, in_specs=in_specs, out_specs=out_specs, check_vma=False
    )
```

```python
import functools

import jax
import jax.numpy as jnp
from jax import lax
from jax.experimental import pallas as pl
from jax.experimental.pallas import tpu as pltpu
from jax.sharding import PartitionSpec as P

decay_rate = 0.3
four_pi = 12.566370614359172
soften = 0.0025
log2_e = 1.4426950408889634
centre = 0.4
MESH = pl.DeviceIdType.MESH


def cut(value):
    first = lax.reduce_precision(value, 8, 7)
    rest = value - first
    second = lax.reduce_precision(rest, 8, 7)
    third = lax.reduce_precision(rest - second, 8, 7)
    return first, second, third


def kernel(
    sizes,
    sketch_ref, spots_ref, feats_ref, logw_ref, hot_ref, keep_ref,
    sums_ref, gram_ref,
    sk_own, sk_got, spots, feats_got, logw_got, hot_got,
    lhs, acc, far_send, far_recv, near_send, near_recv, z_send, z_recv,
    own_sem, sk_send_sem, sk_recv_sem, spot_send_sem, spot_recv_sem, side_send_sem, side_recv_sem,
    far_send_sem, far_recv_sem, near_send_sem, near_recv_sem, z_send_sem, z_recv_sem,
):
    chips, helpers, slots, chunk, chunks, width = sizes
    lines = chips // 2
    half = chunk // 2
    others = helpers - 1
    row = lax.axis_index("row")
    col = lax.axis_index("help")
    chip, core = row // 2, row % 2
    line, side = chip // 2, chip % 2
    sibling = chip * 2 + 1 - core
    peers = chips * helpers

    def chip_at(offset):
        return lax.rem(line + offset // 2, lines) * 2 + lax.rem(side + offset % 2, 2)

    def place(step):
        return (lax.rem(chip + step // helpers, chips), lax.rem(col + step % helpers, helpers))

    def back(step):
        return (
            lax.rem(chip + chips - step // helpers, chips),
            lax.rem(col + helpers - step % helpers, helpers),
        )

    barrier = pltpu.get_barrier_semaphore()

    @pl.loop(1, peers)
    def _(step):
        to_chip, to_col = place(step)
        pl.semaphore_signal(barrier, inc=1, device_id=(to_chip * 2 + core, to_col), device_id_type=MESH)

    pl.semaphore_signal(barrier, inc=1, device_id=(sibling, col), device_id_type=MESH)
    pl.semaphore_wait(barrier, peers)

    def remote(source, target, send_sem, recv_sem, to_row, to_col):
        return pltpu.make_async_remote_copy(
            src_ref=source,
            dst_ref=target,
            send_sem=send_sem,
            recv_sem=recv_sem,
            device_id=(to_row, to_col),
            device_id_type=MESH,
        )

    def spot_copy(step):
        to_chip, to_col = place(step)
        return remote(
            spots_ref, spots.at[chip * helpers + col],
            spot_send_sem.at[step], spot_recv_sem.at[step], to_chip * 2 + core, to_col,
        )

    def spot_arrival(step):
        from_chip, from_col = back(step)
        return remote(
            spots_ref, spots.at[from_chip * helpers + from_col],
            spot_send_sem.at[step], spot_recv_sem.at[step], from_chip * 2 + core, from_col,
        )

    def to_sibling(source, target, index):
        return remote(source, target, side_send_sem.at[index], side_recv_sem.at[index], sibling, col)

    sides = (
        to_sibling(feats_ref, feats_got, 0),
        to_sibling(logw_ref, logw_got, 1),
        to_sibling(hot_ref.at[:, 1 - core], hot_got, 2),
    )

    def sketch_copy(offset):
        group = chip_at(offset)
        return remote(
            sketch_ref.at[group, 1 - core], sk_got.at[group],
            sk_send_sem.at[offset], sk_recv_sem.at[offset], sibling, col,
        )

    def own_copy(offset):
        group = chip_at(offset)
        return pltpu.make_async_copy(sketch_ref.at[group, core], sk_own.at[group], own_sem.at[offset])

    own_spot = pltpu.make_async_copy(spots_ref, spots.at[chip * helpers + col], own_sem.at[chips])
    own_spot.start()

    @pl.loop(1, peers)
    def _(step):
        spot_copy(step).start()

    for each in sides:
        each.start()

    @pl.loop(0, chips)
    def _(turn):
        offset = chips - 1 - turn
        sketch_copy(offset).start()
        own_copy(offset).start()

    lhs[...] = jnp.where(
        lax.broadcasted_iota(jnp.int32, lhs.shape, 1) == 4, jnp.float32(1), jnp.float32(0)
    )
    gram_ref[...] = jnp.zeros_like(gram_ref)
    own_spot.wait()
    for each in sides:
        each.wait()

    @pl.loop(1, peers)
    def _(step):
        spot_copy(step).wait_send()
        spot_arrival(step).wait_recv()

    def rows_of(index):
        return pl.ds(pl.multiple_of(index * chunk, chunk), chunk)

    def block(index, group, sketches, feats, logw, hot_rows, slot, unit):
        spot = jnp.zeros((4, chunk), jnp.float32)
        hots = []
        for step in range(others):
            hot = hot_rows(slot * others + step)
            hots.append(hot)
            target = group * helpers + lax.rem(col + 1 + step, helpers)
            spot = spot + hot[:, :chunk] * spots[target, :, rows_of(index)]
        lhs[unit, 0:4, :] = spot
        full = lhs[unit]
        one = full.astype(jnp.bfloat16).astype(jnp.float32)
        rest = full - one
        two = rest.astype(jnp.bfloat16).astype(jnp.float32)
        three = rest - two
        stack = jnp.concatenate([one, one, two, two, one, three], axis=0)
        left = stack.T.astype(jnp.bfloat16)
        square = jnp.dot(left, feats, preferred_element_type=jnp.float32)
        inverse = lax.rsqrt(square)
        tile = (jnp.exp2(logw - square * inverse) * inverse).astype(jnp.bfloat16)
        product = jnp.dot(tile, sketches, preferred_element_type=jnp.float32)
        return [hot[:, :width] * product for hot in hots]

    def compute(index, offset):
        group = chip_at(offset)
        totals = [None] * others
        for slot in range(slots):
            mine = block(
                index, group, sk_own[group, slot], feats_ref[...], logw_ref[...],
                lambda at: hot_ref[group, core, at], slot, slot,
            )
            theirs = block(
                index, group, sk_got[group, slot], feats_got[...], logw_got[...],
                lambda at: hot_got[group, at], slot, slots + slot,
            )
            for step in range(others):
                part = mine[step] + theirs[step]
                totals[step] = part if totals[step] is None else totals[step] + part
        return totals

    def far_copy(index, way, hop):
        to_chip = chip_at(1) if way == 0 else chip_at(2 * (hop + 1))
        return remote(
            far_send.at[index % 2, way, hop], far_recv.at[index, way, hop],
            far_send_sem.at[index % 2, way, hop], far_recv_sem.at[index, way, hop],
            to_chip * 2 + core, col,
        )

    def near_offset(at):
        return jnp.where(at == lines - 1, 1, 2 * (at + 1))

    def near_copy(index, at):
        return remote(
            near_send.at[index % 2, at], near_recv.at[index, at],
            near_send_sem.at[index % 2, at], near_recv_sem.at[index, at],
            chip_at(near_offset(at)) * 2 + core, col,
        )

    def z_copy(index, step):
        return remote(
            z_send.at[index % 2, step], z_recv.at[index, step],
            z_send_sem.at[index % 2, step], z_recv_sem.at[index, step],
            row, lax.rem(col + 1 + step, helpers),
        )

    def send_far(index):
        @pl.loop(0, lines - 1)
        def _(hop):
            offset = 2 * (hop + 1) + 1

            @pl.when(index == 0)
            def _():
                own_copy(offset).wait()
                sketch_copy(offset).wait()

            @pl.when(index >= 2)
            def _():
                for way in range(2):
                    far_copy(index, way, hop).wait_send()

            totals = compute(index, offset)
            for way in range(2):
                for step in range(others):
                    far_send[index % 2, way, hop, step] = totals[step][
                        way * half : (way + 1) * half
                    ].astype(jnp.bfloat16)
                far_copy(index, way, hop).start()

    def send_near(index):
        @pl.loop(0, lines + 1)
        def _(at):
            offset = jnp.where(at == lines, 0, near_offset(at))

            @pl.when(index == 0)
            def _():
                own_copy(offset).wait()
                sketch_copy(offset).wait()

            totals = compute(index, offset)
            for step in range(others):
                acc[at + jnp.where(at == lines, index % 2, 0), step] = totals[step]

        @pl.when(index >= 2)
        def _():
            @pl.loop(0, lines)
            def _(at):
                near_copy(index, at).wait_send()

        @pl.loop(0, lines - 1)
        def _(hop):
            far_copy(index, 0, hop).wait_recv()
            far_copy(index, 1, hop).wait_recv()
            for step in range(others):
                near_send[index % 2, hop, step, :half] = (
                    acc[hop, step, :half] + far_recv[index, 0, hop, step].astype(jnp.float32)
                ).astype(jnp.bfloat16)
                near_send[index % 2, hop, step, half:] = acc[hop, step, half:].astype(jnp.bfloat16)
                acc[lines - 1, step, half:] += far_recv[index, 1, hop, step].astype(jnp.float32)
            near_copy(index, hop).start()

        for step in range(others):
            near_send[index % 2, lines - 1, step] = acc[lines - 1, step].astype(jnp.bfloat16)
        near_copy(index, lines - 1).start()

    def gather(index):
        @pl.loop(0, lines)
        def _(at):
            near_copy(index, at).wait_recv()

        for step in range(others):
            total = acc[lines + index % 2, step]
            for at in range(lines):
                total = total + near_recv[index, at, step].astype(jnp.float32)

            @pl.when(index >= 2)
            def _():
                z_copy(index, step).wait_send()

            z_send[index % 2, step] = total.astype(jnp.bfloat16)
            z_copy(index, step).start()

    def finish(index):
        total = None
        for step in range(others):
            z_copy(index, step).wait_recv()
            part = z_recv[index, step].astype(jnp.float32)
            total = part if total is None else total + part
        total = jnp.where(keep_ref[...] > 0, total, jnp.zeros_like(total))
        sums_ref[rows_of(index), :] = total
        gram_ref[...] += lax.dot_general(
            total, total, (((0,), (0,)), ((), ())),
            precision=lax.Precision.HIGHEST, preferred_element_type=jnp.float32,
        )

    @pl.loop(0, chunks + 3)
    def _(turn):
        @pl.when(turn < chunks)
        def _():
            send_far(turn)

        @pl.when((turn >= 1) & (turn < chunks + 1))
        def _():
            send_near(turn - 1)

        @pl.when((turn >= 2) & (turn < chunks + 2))
        def _():
            gather(turn - 2)

        @pl.when(turn >= 3)
        def _():
            finish(turn - 3)

    for index in (chunks - 2, chunks - 1):
        @pl.loop(0, lines - 1)
        def _(hop):
            for way in range(2):
                far_copy(index, way, hop).wait_send()

        @pl.loop(0, lines)
        def _(at):
            near_copy(index, at).wait_send()

        for step in range(others):
            z_copy(index, step).wait_send()


def per_device(points, sketch, slots, ranks):
    panels = points.shape[2]
    width = sketch.shape[5]
    groups = sketch.shape[2]
    count = sketch.shape[3]
    helpers = lax.axis_size("help")
    others = helpers - 1
    chips = groups // 2
    chunk = panels // 8
    lines = chips // 2
    half = chunk // 2
    chunks = panels // chunk
    col = lax.axis_index("help")

    scale = decay_rate * log2_e
    spot = (points[0, 0:3] - centre) * scale
    norm = jnp.sum(spot * spot, axis=0, keepdims=True)
    spots = jnp.concatenate([spot, norm], axis=0)
    blank = jnp.zeros((3, panels), jnp.float32)
    right = jnp.concatenate(
        [-2.0 * spot, jnp.ones((1, panels), jnp.float32), norm + soften * scale * scale, blank], axis=0
    )
    one, two, three = cut(right)
    feats = jnp.concatenate([one, two, one, two, three, one], axis=0).astype(jnp.bfloat16)
    logw = jnp.log2(points[0, 3:4]) + jnp.log2(jnp.float32(scale / four_pi))
    step = jnp.where(slots[0, 0] >= 0, (slots[0, 0] - col - 1) % helpers, -1)
    hot = (step[:, :, None] == jnp.arange(others, dtype=jnp.int32)).astype(jnp.float32)
    span = max(width, chunk)
    hot = jnp.broadcast_to(
        hot.reshape(chips, 2, count * others, 1, 1), (chips, 2, count * others, 1, span)
    )
    sizes = (chips, helpers, count, chunk, chunks, width)
    bf16, f32 = jnp.bfloat16, jnp.float32
    vmem = pl.BlockSpec(memory_space=pltpu.VMEM)
    dma = pltpu.SemaphoreType.DMA
    keep = (jnp.arange(width, dtype=jnp.int32)[None, :] < ranks[0]).astype(f32)
    sums, gram = pl.pallas_call(
        functools.partial(kernel, sizes),
        out_shape=(
            jax.ShapeDtypeStruct((panels, width), f32),
            jax.ShapeDtypeStruct((width, width), f32),
        ),
        in_specs=[pl.BlockSpec(memory_space=pl.ANY), vmem, vmem, vmem, vmem, vmem],
        out_specs=(vmem, vmem),
        scratch_shapes=[
            pltpu.VMEM((chips, count, panels, width), bf16),
            pltpu.VMEM((chips, count, panels, width), bf16),
            pltpu.VMEM((chips * helpers, 4, panels), f32),
            pltpu.VMEM((48, panels), bf16),
            pltpu.VMEM((1, panels), f32),
            pltpu.VMEM((chips, count * others, 1, span), f32),
            pltpu.VMEM((2 * count, 8, chunk), f32),
            pltpu.VMEM((lines + 2, others, chunk, width), f32),
            pltpu.VMEM((2, 2, lines - 1, others, half, width), bf16),
            pltpu.VMEM((chunks, 2, lines - 1, others, half, width), bf16),
            pltpu.VMEM((2, lines, others, chunk, width), bf16),
            pltpu.VMEM((chunks, lines, others, chunk, width), bf16),
            pltpu.VMEM((2, others, chunk, width), bf16),
            pltpu.VMEM((chunks, others, chunk, width), bf16),
            dma((chips + 1,)),
            dma((chips,)),
            dma((chips,)),
            dma((chips * helpers,)),
            dma((chips * helpers,)),
            dma((3,)),
            dma((3,)),
            dma((2, 2, lines - 1)),
            dma((chunks, 2, lines - 1)),
            dma((2, lines)),
            dma((chunks, lines)),
            dma((2, others)),
            dma((chunks, others)),
        ],
        compiler_params=pltpu.CompilerParams(
            collective_id=0, has_side_effects=True, vmem_limit_bytes=62 * 1024 * 1024
        ),
    )(
        sketch.reshape(chips, 2, count, panels, width), spots, feats, logw, hot, keep,
    )
    return sums[None], gram[None]


def solution(mesh):
    in_specs = (
        P(("row", "help"), None, None),
        P("row", "help", None, None, None, None),
        P("row", "help", None, None),
        P(("row", "help")),
    )
    out_specs = (P(("row", "help"), None, None), P(("row", "help"), None, None))
    return jax.shard_map(
        per_device, mesh=mesh, in_specs=in_specs, out_specs=out_specs, check_vma=False
    )
```

```python
import functools

import jax
import jax.numpy as jnp
from jax import lax
from jax.experimental import pallas as pl
from jax.experimental.pallas import tpu as pltpu
from jax.sharding import PartitionSpec as P

decay_rate = 0.3
four_pi = 12.566370614359172
soften = 0.0025
log2_e = 1.4426950408889634
centre = 0.4
MESH = pl.DeviceIdType.MESH


def cut(value):
    first = value.astype(jnp.bfloat16).astype(jnp.float32)
    rest = value - first
    second = rest.astype(jnp.bfloat16).astype(jnp.float32)
    return first, second, rest - second


def kernel(
    sizes,
    sketch_ref, points_ref, hot_ref, keep_ref,
    sums_ref, gram_ref,
    spots_ref, right, feats_ref, logw_ref, sk_own, sk_got, spots, feats_got, logw_got, hot_got,
    lhs, acc, far_send, far_recv, near_send, near_recv, z_send, z_recv,
    own_sem, sk_send_sem, sk_recv_sem, spot_send_sem, spot_recv_sem, side_send_sem, side_recv_sem,
    far_send_sem, far_recv_sem, near_send_sem, near_recv_sem, z_send_sem, z_recv_sem,
):
    chips, helpers, slots, chunk, chunks, width = sizes
    lines = chips // 2
    half = chunk // 2
    others = helpers - 1
    row = lax.axis_index("row")
    col = lax.axis_index("help")
    chip, core = row // 2, row % 2
    line, side = chip // 2, chip % 2
    sibling = chip * 2 + 1 - core
    peers = chips * helpers

    def chip_at(offset):
        return lax.rem(line + offset // 2, lines) * 2 + lax.rem(side + offset % 2, 2)

    def place(step):
        return (lax.rem(chip + step // helpers, chips), lax.rem(col + step % helpers, helpers))

    def back(step):
        return (
            lax.rem(chip + chips - step // helpers, chips),
            lax.rem(col + helpers - step % helpers, helpers),
        )

    barrier = pltpu.get_barrier_semaphore()

    @pl.loop(1, peers)
    def _(step):
        to_chip, to_col = place(step)
        pl.semaphore_signal(barrier, inc=1, device_id=(to_chip * 2 + core, to_col), device_id_type=MESH)

    pl.semaphore_signal(barrier, inc=1, device_id=(sibling, col), device_id_type=MESH)

    scale = decay_rate * log2_e
    spot = (points_ref[0:3, :] - centre) * scale
    norm = jnp.sum(spot * spot, axis=0, keepdims=True)
    spots_ref[0:3, :] = spot
    spots_ref[3:4, :] = norm
    right[...] = jnp.zeros_like(right)
    right[0:3, :] = -2.0 * spot
    right[3:4, :] = jnp.ones_like(norm)
    right[4:5, :] = norm + soften * scale * scale
    one, two, three = cut(right[...])
    feats_ref[...] = jnp.concatenate([one, two, one, two, three, one], axis=0).astype(jnp.bfloat16)
    logw_ref[...] = jnp.log(points_ref[3:4, :] * (scale / four_pi)) * log2_e

    pl.semaphore_wait(barrier, peers)

    def remote(source, target, send_sem, recv_sem, to_row, to_col):
        return pltpu.make_async_remote_copy(
            src_ref=source,
            dst_ref=target,
            send_sem=send_sem,
            recv_sem=recv_sem,
            device_id=(to_row, to_col),
            device_id_type=MESH,
        )

    def spot_copy(step):
        to_chip, to_col = place(step)
        return remote(
            spots_ref, spots.at[chip * helpers + col],
            spot_send_sem.at[step], spot_recv_sem.at[step], to_chip * 2 + core, to_col,
        )

    def spot_arrival(step):
        from_chip, from_col = back(step)
        return remote(
            spots_ref, spots.at[from_chip * helpers + from_col],
            spot_send_sem.at[step], spot_recv_sem.at[step], from_chip * 2 + core, from_col,
        )

    def to_sibling(source, target, index):
        return remote(source, target, side_send_sem.at[index], side_recv_sem.at[index], sibling, col)

    sides = (
        to_sibling(feats_ref, feats_got, 0),
        to_sibling(logw_ref, logw_got, 1),
        to_sibling(hot_ref.at[:, 1 - core], hot_got, 2),
    )

    def sketch_copy(offset):
        group = chip_at(offset)
        return remote(
            sketch_ref.at[group, 1 - core], sk_got.at[group],
            sk_send_sem.at[offset], sk_recv_sem.at[offset], sibling, col,
        )

    def own_copy(offset):
        group = chip_at(offset)
        return pltpu.make_async_copy(sketch_ref.at[group, core], sk_own.at[group], own_sem.at[offset])

    own_spot = pltpu.make_async_copy(spots_ref, spots.at[chip * helpers + col], own_sem.at[chips])
    own_spot.start()

    @pl.loop(1, peers)
    def _(step):
        spot_copy(step).start()

    for each in sides:
        each.start()

    @pl.loop(0, chips)
    def _(turn):
        offset = chips - 1 - turn
        sketch_copy(offset).start()
        own_copy(offset).start()

    lhs[...] = jnp.where(
        lax.broadcasted_iota(jnp.int32, lhs.shape, 1) == 4, jnp.float32(1), jnp.float32(0)
    )
    gram_ref[...] = jnp.zeros_like(gram_ref)
    own_spot.wait()
    for each in sides:
        each.wait()

    @pl.loop(1, peers)
    def _(step):
        spot_copy(step).wait_send()
        spot_arrival(step).wait_recv()

    def rows_of(index):
        return pl.ds(pl.multiple_of(index * chunk, chunk), chunk)

    def block(index, group, sketches, feats, logw, hot_rows, slot, unit):
        spot = jnp.zeros((4, chunk), jnp.float32)
        hots = []
        for step in range(others):
            hot = hot_rows(slot * others + step)
            hots.append(hot)
            target = group * helpers + lax.rem(col + 1 + step, helpers)
            spot = spot + hot[:, :chunk] * spots[target, :, rows_of(index)]
        lhs[unit, 0:4, :] = spot
        full = lhs[unit]
        one = full.astype(jnp.bfloat16).astype(jnp.float32)
        rest = full - one
        two = rest.astype(jnp.bfloat16).astype(jnp.float32)
        three = rest - two
        stack = jnp.concatenate([one, one, two, two, one, three], axis=0)
        left = stack.T.astype(jnp.bfloat16)
        square = jnp.dot(left, feats, preferred_element_type=jnp.float32)
        inverse = lax.rsqrt(square)
        tile = (jnp.exp2(logw - square * inverse) * inverse).astype(jnp.bfloat16)
        product = jnp.dot(tile, sketches, preferred_element_type=jnp.float32)
        return [hot[:, :width] * product for hot in hots]

    def compute(index, offset):
        group = chip_at(offset)
        totals = [None] * others
        for slot in range(slots):
            mine = block(
                index, group, sk_own[group, slot], feats_ref[...], logw_ref[...],
                lambda at: hot_ref[group, core, at], slot, slot,
            )
            theirs = block(
                index, group, sk_got[group, slot], feats_got[...], logw_got[...],
                lambda at: hot_got[group, at], slot, slots + slot,
            )
            for step in range(others):
                part = mine[step] + theirs[step]
                totals[step] = part if totals[step] is None else totals[step] + part
        return totals

    def far_copy(index, way, hop):
        to_chip = chip_at(1) if way == 0 else chip_at(2 * (hop + 1))
        return remote(
            far_send.at[index % 2, way, hop], far_recv.at[index, way, hop],
            far_send_sem.at[index % 2, way, hop], far_recv_sem.at[index, way, hop],
            to_chip * 2 + core, col,
        )

    def near_offset(at):
        return jnp.where(at == lines - 1, 1, 2 * (at + 1))

    def near_copy(index, at):
        return remote(
            near_send.at[index % 2, at], near_recv.at[index, at],
            near_send_sem.at[index % 2, at], near_recv_sem.at[index, at],
            chip_at(near_offset(at)) * 2 + core, col,
        )

    def z_copy(index, step):
        return remote(
            z_send.at[index % 2, step], z_recv.at[index, step],
            z_send_sem.at[index % 2, step], z_recv_sem.at[index, step],
            row, lax.rem(col + 1 + step, helpers),
        )

    def send_far(index):
        @pl.loop(0, lines - 1)
        def _(hop):
            offset = 2 * (hop + 1) + 1

            @pl.when(index == 0)
            def _():
                own_copy(offset).wait()
                sketch_copy(offset).wait()

            @pl.when(index >= 2)
            def _():
                for way in range(2):
                    far_copy(index, way, hop).wait_send()

            totals = compute(index, offset)
            for way in range(2):
                for step in range(others):
                    far_send[index % 2, way, hop, step] = totals[step][
                        way * half : (way + 1) * half
                    ].astype(jnp.bfloat16)
                far_copy(index, way, hop).start()

    def send_near(index):
        @pl.loop(0, lines + 1)
        def _(at):
            offset = jnp.where(at == lines, 0, near_offset(at))

            @pl.when(index == 0)
            def _():
                own_copy(offset).wait()
                sketch_copy(offset).wait()

            totals = compute(index, offset)
            for step in range(others):
                acc[at + jnp.where(at == lines, index % 2, 0), step] = totals[step]

        @pl.when(index >= 2)
        def _():
            @pl.loop(0, lines)
            def _(at):
                near_copy(index, at).wait_send()

        @pl.loop(0, lines - 1)
        def _(hop):
            far_copy(index, 0, hop).wait_recv()
            far_copy(index, 1, hop).wait_recv()
            for step in range(others):
                near_send[index % 2, hop, step, :half] = (
                    acc[hop, step, :half] + far_recv[index, 0, hop, step].astype(jnp.float32)
                ).astype(jnp.bfloat16)
                near_send[index % 2, hop, step, half:] = acc[hop, step, half:].astype(jnp.bfloat16)
                acc[lines - 1, step, half:] += far_recv[index, 1, hop, step].astype(jnp.float32)
            near_copy(index, hop).start()

        for step in range(others):
            near_send[index % 2, lines - 1, step] = acc[lines - 1, step].astype(jnp.bfloat16)
        near_copy(index, lines - 1).start()

    def gather(index):
        @pl.loop(0, lines)
        def _(at):
            near_copy(index, at).wait_recv()

        for step in range(others):
            total = acc[lines + index % 2, step]
            for at in range(lines):
                total = total + near_recv[index, at, step].astype(jnp.float32)

            @pl.when(index >= 2)
            def _():
                z_copy(index, step).wait_send()

            z_send[index % 2, step] = total.astype(jnp.bfloat16)
            z_copy(index, step).start()

    def finish(index):
        total = None
        for step in range(others):
            z_copy(index, step).wait_recv()
            part = z_recv[index, step].astype(jnp.float32)
            total = part if total is None else total + part
        total = jnp.where(keep_ref[...] > 0, total, jnp.zeros_like(total))
        sums_ref[rows_of(index), :] = total
        gram_ref[...] += lax.dot_general(
            total, total, (((0,), (0,)), ((), ())),
            precision=lax.Precision.HIGHEST, preferred_element_type=jnp.float32,
        )

    @pl.loop(0, chunks + 3)
    def _(turn):
        @pl.when(turn < chunks)
        def _():
            send_far(turn)

        @pl.when((turn >= 1) & (turn < chunks + 1))
        def _():
            send_near(turn - 1)

        @pl.when((turn >= 2) & (turn < chunks + 2))
        def _():
            gather(turn - 2)

        @pl.when(turn >= 3)
        def _():
            finish(turn - 3)

    for index in (chunks - 2, chunks - 1):
        @pl.loop(0, lines - 1)
        def _(hop):
            for way in range(2):
                far_copy(index, way, hop).wait_send()

        @pl.loop(0, lines)
        def _(at):
            near_copy(index, at).wait_send()

        for step in range(others):
            z_copy(index, step).wait_send()


def per_device(points, sketch, slots, ranks):
    panels = points.shape[2]
    width = sketch.shape[5]
    groups = sketch.shape[2]
    count = sketch.shape[3]
    helpers = lax.axis_size("help")
    others = helpers - 1
    chips = groups // 2
    chunk = panels // 8
    lines = chips // 2
    half = chunk // 2
    chunks = panels // chunk
    col = lax.axis_index("help")

    step = jnp.where(slots[0, 0] >= 0, (slots[0, 0] - col - 1) % helpers, -1)
    hot = (step[:, :, None] == jnp.arange(others, dtype=jnp.int32)).astype(jnp.float32)
    span = max(width, chunk)
    hot = jnp.broadcast_to(
        hot.reshape(chips, 2, count * others, 1, 1), (chips, 2, count * others, 1, span)
    )
    sizes = (chips, helpers, count, chunk, chunks, width)
    bf16, f32 = jnp.bfloat16, jnp.float32
    vmem = pl.BlockSpec(memory_space=pltpu.VMEM)
    dma = pltpu.SemaphoreType.DMA
    keep = (jnp.arange(width, dtype=jnp.int32)[None, :] < ranks[0]).astype(f32)
    sums, gram = pl.pallas_call(
        functools.partial(kernel, sizes),
        out_shape=(
            jax.ShapeDtypeStruct((panels, width), f32),
            jax.ShapeDtypeStruct((width, width), f32),
        ),
        in_specs=[pl.BlockSpec(memory_space=pl.ANY), vmem, vmem, vmem],
        out_specs=(vmem, vmem),
        scratch_shapes=[
            pltpu.VMEM((4, panels), f32),
            pltpu.VMEM((8, panels), f32),
            pltpu.VMEM((48, panels), bf16),
            pltpu.VMEM((1, panels), f32),
            pltpu.VMEM((chips, count, panels, width), bf16),
            pltpu.VMEM((chips, count, panels, width), bf16),
            pltpu.VMEM((chips * helpers, 4, panels), f32),
            pltpu.VMEM((48, panels), bf16),
            pltpu.VMEM((1, panels), f32),
            pltpu.VMEM((chips, count * others, 1, span), f32),
            pltpu.VMEM((2 * count, 8, chunk), f32),
            pltpu.VMEM((lines + 2, others, chunk, width), f32),
            pltpu.VMEM((2, 2, lines - 1, others, half, width), bf16),
            pltpu.VMEM((chunks, 2, lines - 1, others, half, width), bf16),
            pltpu.VMEM((2, lines, others, chunk, width), bf16),
            pltpu.VMEM((chunks, lines, others, chunk, width), bf16),
            pltpu.VMEM((2, others, chunk, width), bf16),
            pltpu.VMEM((chunks, others, chunk, width), bf16),
            dma((chips + 1,)),
            dma((chips,)),
            dma((chips,)),
            dma((chips * helpers,)),
            dma((chips * helpers,)),
            dma((3,)),
            dma((3,)),
            dma((2, 2, lines - 1)),
            dma((chunks, 2, lines - 1)),
            dma((2, lines)),
            dma((chunks, lines)),
            dma((2, others)),
            dma((chunks, others)),
        ],
        compiler_params=pltpu.CompilerParams(
            collective_id=0, has_side_effects=True, vmem_limit_bytes=62 * 1024 * 1024
        ),
    )(
        sketch.reshape(chips, 2, count, panels, width), points[0], hot, keep,
    )
    return sums[None], gram[None]


def solution(mesh):
    in_specs = (
        P(("row", "help"), None, None),
        P("row", "help", None, None, None, None),
        P("row", "help", None, None),
        P(("row", "help")),
    )
    out_specs = (P(("row", "help"), None, None), P(("row", "help"), None, None))
    return jax.shard_map(
        per_device, mesh=mesh, in_specs=in_specs, out_specs=out_specs, check_vma=False
    )
```
